32 devices in a mesh: rep: 4 (over y, core), dp: 8 (over z, x).
Axes of the slice: x: 2, y: 2, z: 4, core: 2. Of those that a mesh axis runs over, the one named last changes fastest.
Arguments:
- first_core: float32 [512, 512], P('dp'), may hold values from -6 to 6
- first_moment: float32 [512, 512], P('dp'), may hold values from -4 to 4
- first_second: float32 [512, 512], P('dp'), may hold values from 0.01 to 1
- mid_core: float32 [256, 131072], P('dp'), may hold values from -0.5 to 0.5
- mid_moment: float32 [256, 131072], P('dp'), may hold values from -4 to 4
- mid_second: float32 [256, 131072], P('dp'), may hold values from 0.01 to 1
- last_core: float32 [512, 512], P('dp'), may hold values from -0.5 to 0.5
- last_moment: float32 [512, 512], P('dp'), may hold values from -4 to 4
- last_second: float32 [512, 512], P('dp'), may hold values from 0.01 to 1
- cotangent: bfloat16 [512, 128], P(('rep', 'dp')), may hold values from -6 to 6
- bag_lengths: int32 [32, 16], P(('rep', 'dp')), may hold values from 1 to 32, 256 in all within a row
- first_digit: int32 [8192], P(('rep', 'dp')), may hold values from 0 to 511
- mid_digit: int32 [8192, 1], P(('rep', 'dp')), may hold values from 0 to 255; in each aligned block of 256 rows (0 to 255, 256 to 511, ...) at most 2 rows name the same one
- last_digit: int32 [8192], P(('rep', 'dp')), may hold values from 0 to 511
Outputs:
- first_core_next: float32 [512, 512], P('dp')
- first_moment_next: float32 [512, 512], P('dp')
- first_second_next: float32 [512, 512], P('dp')
- mid_core_next: float32 [256, 131072], P('dp')
- mid_moment_next: float32 [256, 131072], P('dp')
- mid_second_next: float32 [256, 131072], P('dp')
- last_core_next: float32 [512, 512], P('dp')
- last_moment_next: float32 [512, 512], P('dp')
- last_second_next: float32 [512, 512], P('dp')
The draws below stay inside these ranges and needn't reach their ends.
Inputs may be any that keep to these rules, and one draw needn't show every extreme that they name: `mid_digit`: within each block of 256 lookups no middle digit appears more than 2 times, and in some block one digit appears exactly 2 times. `bag_lengths`: each row sums to 256; some entry of each row equals 32.
All inputs are finite; a program needn't handle non-finite values.
Results may differ from the reference program's by a relative error of at most 0.0056.
Values may be sent and summed in bfloat16 or wider, within the bound.
A program may use at most 192 MiB of HBM per device.

```python
import math
import jax
import jax.numpy as jnp
import numpy as np
from jax import lax

N1 = 512
N2 = 256
N3 = 512
R = 128
D1 = 4
D2 = 8
D3 = 4
STEP = 20
SAMP_DEV = 16
D = 128
LK_DEV = 256
MOSTLEN = 32
CAP = 2
SAMPLES = 512
LOOKUPS = 8192
N_REP = 4
N_DP = 8


def set_ends(array, rng, low, top_value):
    shape = array.shape
    spot = [jax.random.randint(jax.random.fold_in(rng, axis), (), 0, shape[axis]) for axis in range(len(shape))]
    array = array.at[tuple(spot)].set(low)
    longest = shape.index(max(shape))
    spot[longest] = (spot[longest] + 1) % shape[longest]
    return array.at[tuple(spot)].set(top_value)


def levels(own_key, shape, split, smallest, top_value):
    def one(dim, parts):
        steps = jax.random.uniform(jax.random.fold_in(jax.random.fold_in(own_key, 6), dim), (parts,), jnp.float32, smallest / len(split), top_value / len(split))
        return jnp.repeat(jnp.exp(steps), shape[dim] // parts).reshape((-1,) + (1,) * (len(shape) - dim - 1))

    gain = one(*split[0])
    for cut in split[1:]:
        gain = gain * one(*cut)
    return gain


def cumulative_ranks(count, slope):
    loads = [(1 << 20) // math.isqrt(rank ** slope) + 1 for rank in range(1, count + 1)]
    scale = 1 + sum(loads) // (1 << 30)
    return np.cumsum(np.array([max(1, weight // scale) for weight in loads]))


def ranked_ids(rng, shape, count, skew):
    listing = cumulative_ranks(count, skew)
    pick = jax.random.randint(jax.random.fold_in(rng, 1), shape, 0, int(listing[count - 1]))
    standing = jnp.searchsorted(jnp.asarray(listing, jnp.int32), pick, side="right")
    return jax.random.permutation(jax.random.fold_in(rng, 2), count)[standing].astype(jnp.int32)


def split_up(amount, total, bound, skew):
    loads = [(1 << 20) // math.isqrt(standing ** skew) + 1 for standing in range(2, amount + 1)]
    spare, given = total - bound - (amount - 1), [1] * (amount - 1)
    while spare > 0:
        candidates = [i for i in range(amount - 1) if given[i] < bound]
        mass, left = sum([loads[i] for i in candidates]), spare
        for i in candidates:
            addition = min(bound - given[i], max(1, left * loads[i] // mass), spare)
            given[i] = given[i] + addition
            spare = spare - addition
    return np.array([bound] + given)


def uneven_parts(rng, number_of, total, most, lean):
    if number_of == 2:
        one = jax.random.randint(rng, (), max(1, total - most), min(most, total - 1) + 1)
        return jnp.stack([one, total - one])
    tallies = jnp.asarray(split_up(number_of, total, most, lean), jnp.int32)
    couples = (number_of - 1) // 2
    giver, taker = tallies[1:1 + 2 * couples:2], tallies[2:2 + 2 * couples:2]
    room = jnp.minimum(giver - 1, most - taker)
    passed = jax.random.randint(jax.random.fold_in(rng, 1), (couples,), 0, 1 << 20) % (room + 1)
    tallies = tallies.at[1:1 + 2 * couples:2].set(giver - passed).at[2:2 + 2 * couples:2].set(taker + passed)
    return tallies[jax.random.permutation(jax.random.fold_in(rng, 2), number_of)]


def shared_out(rng, own, number, rows, number_of, top, most, skew):
    ranking = jax.random.permutation(rng, number_of)
    packed, usual = load_shares(number_of, rows * top, most, skew, True), load_shares(number_of, rows * top, most, skew, False)
    places = jnp.arange(number_of)

    def named(tallies, offset_by):
        used = int((tallies > 0).sum())
        fixed = max(1, used // 4)
        passed = fixed + (places - fixed + offset_by * (used - fixed)) % max(1, number_of - fixed)
        return jnp.zeros((number_of,), jnp.int32).at[ranking[jnp.where(places < fixed, places, passed)]].set(jnp.asarray(tallies, jnp.int32))

    tallies = jnp.where(number % 4 == 0, named(packed, number // 4), named(usual, number - number // 4 - 1))
    mixed = jax.random.permutation(jax.random.fold_in(own, 3), number_of)
    giver, sink = mixed[0:number_of // 2 * 2:2], mixed[1:number_of // 2 * 2:2]
    room = jnp.minimum(tallies[giver] - 1, most - tallies[sink]) // 2
    room = jnp.where((giver == ranking[0]) | (sink == ranking[0]) | (tallies[sink] == 0), 0, jnp.maximum(room, 0))
    passed = jax.random.randint(jax.random.fold_in(own, 4), (number_of // 2,), 0, 1 << 20) % (room + 1)
    tallies = tallies.at[giver].add(-passed).at[sink].add(passed)
    members = jnp.searchsorted(jnp.cumsum(tallies), jnp.arange(rows * top), side="right").astype(jnp.int32)
    listing = members.reshape(top, rows).T
    listing = listing[jax.random.permutation(jax.random.fold_in(own, 1), rows)]
    offset_by = jax.random.randint(jax.random.fold_in(own, 2), (rows, 1), 0, top)
    return jnp.take_along_axis(listing, (jnp.arange(top)[None, :] + offset_by) % top, axis=1)


def load_shares(amount, total, limit, slope, full):
    weights = [(1 << 20) // math.isqrt(rank ** slope) + 1 for rank in range(1, amount + 1)]
    largest = limit if full else min(limit, max(-(-total // amount), total * weights[0] // sum(weights)))
    least = 1 if total - largest >= amount - 1 else 0
    holding, rest = [largest] + [least] * (amount - 1), total - largest - least * (amount - 1)
    while rest > 0:
        candidates = [i for i in range(1, amount) if holding[i] < largest] or [i for i in range(1, amount) if holding[i] < limit]
        mass, budget = sum([weights[i] for i in candidates]), rest
        for i in candidates:
            addition = min(limit - holding[i], max(1, budget * weights[i] // mass), rest)
            holding[i] = holding[i] + addition
            rest = rest - addition
    return np.array(holding)


def gaussian(own_key, dims, deviation, bound, cuts=(), kind=jnp.bfloat16):
    values = jax.random.normal(own_key, dims, jnp.float32) * deviation
    if len(cuts) > 0:
        values = levels(own_key, dims, cuts, -0.22, 0.18) * values
    return jnp.clip(values, min=-bound, max=bound).astype(kind)


def setup_inputs(seed: int = 0) -> dict:
    key_of = jax.random.split(jax.random.key(seed), 15)
    first_core = gaussian(key_of[0], (N1, D1 * R), 1.0, 6.0, ((0, 8),), jnp.float32)
    first_moment = gaussian(key_of[1], (N1, D1 * R), 0.5, 4.0, ((0, 8),), jnp.float32)
    first_second = jnp.clip(jnp.exp(math.log(1.0) - 4.6051702 * jax.random.uniform(key_of[2], (N1, D1 * R), jnp.float32) ** levels(key_of[2], (N1, D1 * R), ((0, 8),), -0.2, 0.2)), 0.01, 1.0)
    mid_core = gaussian(key_of[3], (N2, R * D2 * R), R ** -0.5, 0.5, ((0, 8),), jnp.float32)
    mid_moment = gaussian(key_of[4], (N2, R * D2 * R), 0.5, 4.0, ((0, 8),), jnp.float32)
    mid_second = jnp.clip(jnp.exp(math.log(1.0) - 4.6051702 * jax.random.uniform(key_of[5], (N2, R * D2 * R), jnp.float32) ** levels(key_of[5], (N2, R * D2 * R), ((0, 8),), -0.2, 0.2)), 0.01, 1.0)
    last_core = gaussian(key_of[6], (N3, R * D3), R ** -0.5, 0.5, ((0, 8),), jnp.float32)
    last_moment = gaussian(key_of[7], (N3, R * D3), 0.5, 4.0, ((0, 8),), jnp.float32)
    last_second = jnp.clip(jnp.exp(math.log(1.0) - 4.6051702 * jax.random.uniform(key_of[8], (N3, R * D3), jnp.float32) ** levels(key_of[8], (N3, R * D3), ((0, 8),), -0.2, 0.2)), 0.01, 1.0)
    cotangent = gaussian(key_of[9], (SAMPLES, D), 1.0, 6.0, ((0, 32),))
    bag_lengths = jax.vmap(lambda own: uneven_parts(own, SAMP_DEV, LK_DEV, MOSTLEN, 1))(jax.random.split(key_of[10], (N_REP * N_DP))).reshape((N_REP * N_DP, SAMP_DEV)).astype(jnp.int32)
    first_digit = set_ends(ranked_ids(key_of[11], (LOOKUPS,), N1, 1), jax.random.fold_in(key_of[11], 3), 0, N1 - 1).astype(jnp.int32)
    mid_digit_keys = jax.random.split(jax.random.fold_in(key_of[12], 1), LOOKUPS // LK_DEV)
    mid_digit_turns = jax.random.permutation(jax.random.fold_in(key_of[12], 3), LOOKUPS // LK_DEV)
    mid_digit = jax.vmap(lambda own, number: shared_out(jax.random.fold_in(key_of[12], 2), own, number, LK_DEV, N2, 1, CAP, 1))(mid_digit_keys, mid_digit_turns).reshape((LOOKUPS, 1))
    last_digit = set_ends(ranked_ids(key_of[13], (LOOKUPS,), N3, 1), jax.random.fold_in(key_of[13], 3), 0, N3 - 1).astype(jnp.int32)
    return {"first_core": first_core, "first_moment": first_moment, "first_second": first_second, "mid_core": mid_core, "mid_moment": mid_moment, "mid_second": mid_second, "last_core": last_core, "last_moment": last_moment, "last_second": last_second, "cotangent": cotangent, "bag_lengths": bag_lengths, "first_digit": first_digit, "mid_digit": mid_digit, "last_digit": last_digit}


LEARN_RATE = 0.01
BETA_ONE = 0.9
BETA_TWO = 0.999
EPSILON = 1e-08

def adam_update(current, moment, second, gradient):
    moment_next = BETA_ONE * moment + (1.0 - BETA_ONE) * gradient
    second_next = BETA_TWO * second + (1.0 - BETA_TWO) * gradient * gradient
    corrected = moment_next / (1.0 - BETA_ONE ** STEP)
    spread = jnp.sqrt(second_next / (1.0 - BETA_TWO ** STEP))
    return (current - LEARN_RATE * corrected / (spread + EPSILON), moment_next, second_next)

def reference(first_core, first_moment, first_second, mid_core, mid_moment, mid_second, last_core, last_moment, last_second, cotangent, bag_lengths, first_digit, mid_digit, last_digit):
    blocks = bag_lengths.shape[0]
    look_count = first_digit.shape[0] // blocks
    positions = jnp.arange(look_count, dtype=jnp.int32)
    bag_ends = jnp.cumsum(bag_lengths, axis=1)
    sample_of = lax.optimization_barrier(jnp.sum((bag_ends[:, None, :] <= positions[None, :, None]).astype(jnp.int32), axis=2))
    sample_of = sample_of + (jnp.arange(blocks, dtype=jnp.int32) * SAMP_DEV)[:, None]
    lookup_grads = cotangent[sample_of.reshape(-1)]
    mid_rows = mid_digit[:, 0].reshape(blocks, look_count)

    def block_rank(row_ids):
        earlier = (row_ids[None, :] == row_ids[:, None]) & (positions[None, :] < positions[:, None])
        return lax.optimization_barrier(jnp.sum(earlier.astype(jnp.int32), axis=1))
    slot_rank = lax.map(block_rank, mid_rows)
    slot_index = (mid_rows * blocks + jnp.arange(blocks, dtype=jnp.int32)[:, None]) * CAP + slot_rank
    lookup_ids = jnp.arange(first_digit.shape[0], dtype=jnp.int32) + 1
    owner_of = jnp.zeros((N2 * blocks * CAP,), jnp.int32).at[slot_index.reshape(-1)].set(lookup_ids)
    owner_of = owner_of.reshape(N2, blocks * CAP)
    first_copy = first_core.astype(jnp.bfloat16)
    mid_copy = mid_core.astype(jnp.bfloat16)
    last_copy = last_core.astype(jnp.bfloat16)

    def row_step(totals, row_items):
        first_acc, last_acc = totals
        slot_owner, mid_row = row_items
        live_slot = slot_owner > 0
        picked = jnp.maximum(slot_owner - 1, 0)
        slot_count = slot_owner.shape[0]
        slot_grads = jnp.where(live_slot[:, None], lookup_grads[picked], jnp.zeros((), jnp.bfloat16))
        slot_first = jnp.where(live_slot, first_digit[picked], 0).astype(jnp.int32)
        slot_last = jnp.where(live_slot, last_digit[picked], 0).astype(jnp.int32)
        grad_cube = slot_grads.reshape(slot_count, D1, D2, D3).astype(jnp.float32)
        first_rows = first_copy[slot_first].reshape(slot_count, D1, R).astype(jnp.float32)
        last_rows = last_copy[slot_last].reshape(slot_count, R, D3).astype(jnp.float32)
        mid_cube = mid_row.reshape(R, D2, R).astype(jnp.float32)
        first_mix = jnp.einsum('kar,kabc->krbc', first_rows, grad_cube).astype(jnp.bfloat16)
        mid_term = jnp.einsum('krbc,ksc->rbs', first_mix.astype(jnp.float32), last_rows)
        tail_mix = jnp.einsum('rbs,ksc->krbc', mid_cube, last_rows).astype(jnp.bfloat16)
        first_term = jnp.einsum('kabc,krbc->kar', grad_cube, tail_mix.astype(jnp.float32))
        head_mix = jnp.einsum('kar,rbs->kabs', first_rows, mid_cube).astype(jnp.bfloat16)
        last_term = jnp.einsum('kabs,kabc->ksc', head_mix.astype(jnp.float32), grad_cube)
        first_acc = first_acc + jax.ops.segment_sum(first_term.reshape(slot_count, D1 * R), slot_first, num_segments=N1)
        last_acc = last_acc + jax.ops.segment_sum(last_term.reshape(slot_count, R * D3), slot_last, num_segments=N3)
        return ((first_acc, last_acc), mid_term.reshape(-1))
    start = (jnp.zeros((N1, D1 * R), jnp.float32), jnp.zeros((N3, R * D3), jnp.float32))
    (first_grad, last_grad), mid_grad = lax.scan(row_step, start, (owner_of, mid_copy))
    first_next = adam_update(first_core, first_moment, first_second, first_grad)
    mid_next = adam_update(mid_core, mid_moment, mid_second, mid_grad)
    last_next = adam_update(last_core, last_moment, last_second, last_grad)
    return (first_next[0], first_next[1], first_next[2], mid_next[0], mid_next[1], mid_next[2], last_next[0], last_next[1], last_next[2])
```

```python
import jax
import jax.numpy as jnp
from jax import lax
from jax.experimental import pallas as pl
from jax.experimental.pallas import tpu as pltpu
from jax.sharding import PartitionSpec as P

R = 128
D1 = 4
D2 = 8
D3 = 4
STEP = 20
CAP = 2
GROUP_ROWS = 8
RCHUNK = 16
LANES = RCHUNK * D2

LEARN_RATE = 0.01
BETA_ONE = 0.9
BETA_TWO = 0.999
EPSILON = 1e-08

F32 = jnp.float32
BF16 = jnp.bfloat16


def adam_update(current, moment, second, gradient):
    moment_next = BETA_ONE * moment + (1.0 - BETA_ONE) * gradient
    second_next = BETA_TWO * second + (1.0 - BETA_TWO) * gradient * gradient
    corrected = moment_next * (LEARN_RATE / (1.0 - BETA_ONE**STEP))
    spread = jnp.sqrt(second_next * (1.0 / (1.0 - BETA_TWO**STEP)))
    return (current - corrected / (spread + EPSILON), moment_next, second_next)


def contract(left, right, left_dim, right_dim):
    return lax.dot_general(
        left, right, (((left_dim,), (right_dim,)), ((), ())), preferred_element_type=F32
    )


def mid_kernel(group, slots, part_ref, g_ref, f_ref, l_ref, core_ref, moment_ref, second_ref,
               core_out, moment_out, second_out, first_out, last_out,
               grad_wide, first_wide, mix, core_rows, grad_rows, first_wide_terms):
    chunk = pl.program_id(1)
    part = part_ref[0]
    row_id = lax.broadcasted_iota(jnp.int32, (R, LANES), 0)
    lane_id = lax.broadcasted_iota(jnp.int32, (R, LANES), 1)

    @pl.when(chunk == 0)
    def _():
        grads = g_ref[...]
        for a in range(D1):
            for c in range(D3):
                spread = (row_id == a * D2 * D3 + (lane_id % D2) * D3 + c).astype(F32).astype(BF16)
                grad_wide[a * D3 + c] = contract(grads, spread, 1, 0).astype(BF16)
        first_out[...] = jnp.zeros_like(first_out)
        last_out[...] = jnp.zeros_like(last_out)

    for tile in range(LANES):
        core_rows[tile * group:(tile + 1) * group, :] = core_ref[:, tile * R:(tile + 1) * R]
    pick = (row_id == chunk * RCHUNK + lane_id // D2).astype(F32).astype(BF16)
    for a in range(D1):
        first_wide[a] = contract(f_ref[:, a * R:(a + 1) * R], pick, 1, 0)

    for row in range(group):
        own = slice(row * slots, (row + 1) * slots)
        for c in range(D3):
            total = first_wide[0, own] * grad_wide[c, own].astype(F32)
            for a in range(1, D1):
                total += first_wide[a, own] * grad_wide[a * D3 + c, own].astype(F32)
            mix[row, c] = total.astype(BF16)
        first_mix = mix[row].reshape(D3 * slots, LANES)
        last_rows = jnp.concatenate(
            [l_ref[own, c * R:(c + 1) * R] for c in range(D3)], axis=0
        )
        grad_rows[pl.ds(row, LANES, stride=group), :] = contract(first_mix, last_rows, 0, 0)
        core_row = core_rows[pl.ds(row, LANES, stride=group), :].astype(BF16)
        tail = contract(last_rows, core_row, 1, 1)
        terms = grad_wide[part * D3, own].astype(F32) * tail[:slots]
        for c in range(1, D3):
            terms += (
                grad_wide[part * D3 + c, own].astype(F32) * tail[c * slots:(c + 1) * slots]
            )
        first_wide_terms[own, :] = terms.astype(BF16)
        last_out[own, :] += contract(mix[row, part], core_row, 1, 0)
    first_out[...] += contract(first_wide_terms[...], pick, 1, 1)

    for tile in range(LANES):
        cols = slice(tile * R, (tile + 1) * R)
        core_next, moment_next, second_next = adam_update(
            core_ref[:, cols], moment_ref[:, cols], second_ref[:, cols],
            grad_rows[tile * group:(tile + 1) * group, :],
        )
        core_out[:, cols] = core_next
        moment_out[:, cols] = moment_next
        second_out[:, cols] = second_next


def mid_step(part, grads, firsts, lasts, core, moment, second):
    rows, columns = core.shape
    slots = grads.shape[0] // rows
    group = min(GROUP_ROWS, rows)
    held = group * slots
    chunks = R // RCHUNK
    state = pl.BlockSpec((group, RCHUNK * D2 * R), lambda g, j: (g, j))
    terms = pl.BlockSpec((held, R), lambda g, j: (g, 0))
    wide = pl.BlockSpec((held, D1 * R), lambda g, j: (g, 0))
    return pl.pallas_call(
        lambda *refs: mid_kernel(group, slots, *refs),
        grid=(rows // group, chunks),
        in_specs=[
            pl.BlockSpec(memory_space=pltpu.SMEM), terms, wide, wide, state, state, state,
        ],
        out_specs=[state, state, state, terms, terms],
        out_shape=[jax.ShapeDtypeStruct((rows, columns), F32)] * 3
        + [jax.ShapeDtypeStruct((rows * slots, R), F32)] * 2,
        scratch_shapes=[
            pltpu.VMEM((D1 * D3, held, LANES), BF16),
            pltpu.VMEM((D1, held, LANES), F32),
            pltpu.VMEM((group, D3, slots, LANES), BF16),
            pltpu.VMEM((LANES * group, R), F32),
            pltpu.VMEM((LANES * group, R), F32),
            pltpu.VMEM((held, LANES), BF16),
        ],
        compiler_params=pltpu.CompilerParams(vmem_limit_bytes=56 * 1024 * 1024),
    )(part, grads, firsts, lasts, core, moment, second)


def local(
    first_core, first_moment, first_second,
    mid_core, mid_moment, mid_second,
    last_core, last_moment, last_second,
    cotangent, bag_lengths, first_digit, mid_digit, last_digit,
):
    dp_count = lax.axis_size("dp")
    rep_count = lax.axis_size("rep")
    local_rows = mid_core.shape[0]
    block_samples, embed_dim = cotangent.shape
    look_count = first_digit.shape[0]
    outer_rows = first_core.shape[0] * dp_count

    positions = jnp.arange(look_count, dtype=jnp.int32)
    samples = jnp.arange(block_samples, dtype=jnp.int32)
    bag_ends = jnp.sum(
        jnp.where(samples[None, :] <= samples[:, None], bag_lengths[0][None, :], 0), axis=1
    )
    sample_of = jnp.sum((bag_ends[:, None] <= positions[None, :]).astype(jnp.int32), axis=0)
    pieces = jnp.stack(
        [
            mid_digit[:, 0],
            first_digit // 2,
            last_digit // 2,
            sample_of * 4 + (first_digit % 2) * 2 + last_digit % 2,
        ]
    )
    packed = jnp.concatenate([cotangent, pieces.astype(BF16).reshape(-1, embed_dim)], axis=0)
    packed_all = lax.all_gather(packed, ("rep", "dp"), axis=0, tiled=False)

    column = jnp.arange(R * D3, dtype=jnp.int32)
    reorder = ((column[:, None] % D3) * R + column[:, None] // D3 == column[None, :]).astype(F32)
    last_wide = jnp.dot(
        last_core.astype(BF16), reorder.astype(BF16), preferred_element_type=F32
    ).astype(BF16)
    cores = lax.all_gather(
        jnp.concatenate([first_core.astype(BF16), last_wide], axis=1), "dp", axis=0, tiled=True
    )

    blocks = packed_all.shape[0]
    grads_all = packed_all[:, :block_samples].reshape(blocks * block_samples, embed_dim)
    numbers = packed_all[:, block_samples:].reshape(blocks, 4, look_count).astype(jnp.int32)
    rest = numbers[:, 3]
    keys = (
        (rest // 4) * (outer_rows * outer_rows)
        + (numbers[:, 1] * 2 + (rest // 2) % 2) * outer_rows
        + numbers[:, 2] * 2 + rest % 2
    )
    own_digits = lax.axis_index("dp") * local_rows + jnp.arange(local_rows, dtype=jnp.int32)
    match = numbers[:, 0][None] == own_digits[:, None, None]
    big = jnp.int32(2**30)
    low = jnp.min(jnp.where(match, keys[None], big), axis=2)
    high = jnp.max(jnp.where(match, keys[None], -1), axis=2)
    count = jnp.sum(match.astype(jnp.int32), axis=2)
    slot_keys = jnp.concatenate([jnp.where(count >= 1, low, -1), jnp.where(count >= 2, high, -1)], 1)
    slot_block = jnp.arange(CAP * blocks, dtype=jnp.int32) % blocks
    valid = slot_keys >= 0
    slot_keys = jnp.maximum(slot_keys, 0)
    slot_sample = jnp.where(
        valid, slot_keys // (outer_rows * outer_rows) + slot_block[None, :] * block_samples, -1
    ).reshape(-1)
    slot_first = ((slot_keys // outer_rows) % outer_rows).reshape(-1)
    slot_last = (slot_keys % outer_rows).reshape(-1)

    def one_hot(index, size):
        return (index[:, None] == jnp.arange(size, dtype=jnp.int32)[None, :]).astype(BF16)

    first_hot = one_hot(slot_first, outer_rows)
    last_hot = one_hot(slot_last, outer_rows)
    grads = jnp.dot(
        one_hot(slot_sample, blocks * block_samples), grads_all, preferred_element_type=F32
    ).astype(BF16)
    firsts = jnp.dot(first_hot, cores[:, : D1 * R], preferred_element_type=F32).astype(BF16)
    lasts = jnp.dot(last_hot, cores[:, D1 * R :], preferred_element_type=F32).astype(BF16)

    part = lax.axis_index("rep").astype(jnp.int32).reshape(1)
    core_next, moment_next, second_next, first_terms, last_terms = mid_step(
        part, grads, firsts, lasts, mid_core, mid_moment, mid_second
    )
    partial = jnp.concatenate(
        [
            contract(first_hot, first_terms.astype(BF16), 0, 0),
            contract(last_hot, last_terms.astype(BF16), 0, 0),
        ],
        axis=1,
    ).astype(BF16)
    partial = partial.reshape(dp_count, outer_rows // dp_count, 2 * R)
    arrived = lax.all_to_all(partial, "dp", split_axis=0, concat_axis=0, tiled=True)
    summed = jnp.sum(arrived.astype(F32), axis=0)
    whole = lax.all_gather(summed, "rep", axis=0, tiled=False)
    first_grad = jnp.concatenate([whole[q, :, :R] for q in range(rep_count)], axis=1)
    last_grad = lax.dot_general(
        jnp.concatenate([whole[q, :, R:] for q in range(rep_count)], axis=1),
        reorder,
        (((1,), (1,)), ((), ())),
        precision=lax.Precision.HIGHEST,
        preferred_element_type=F32,
    )
    first_next = adam_update(first_core, first_moment, first_second, first_grad)
    last_next = adam_update(last_core, last_moment, last_second, last_grad)
    return (*first_next, core_next, moment_next, second_next, *last_next)


def solution(mesh):
    core = P("dp", None)
    both = P(("rep", "dp"), None)
    return jax.shard_map(
        local,
        mesh=mesh,
        in_specs=(core,) * 9 + (both, both, P(("rep", "dp")), both, P(("rep", "dp"))),
        out_specs=(core,) * 9,
        check_vma=False,
    )
```

```python
import jax
import jax.numpy as jnp
from jax import lax
from jax.experimental import pallas as pl
from jax.experimental.pallas import tpu as pltpu
from jax.sharding import PartitionSpec as P

R = 128
D1 = 4
D2 = 8
D3 = 4
STEP = 20
CAP = 2
GROUP_ROWS = 8
RCHUNK = 16
LANES = RCHUNK * D2

LEARN_RATE = 0.01
BETA_ONE = 0.9
BETA_TWO = 0.999
EPSILON = 1e-08

F32 = jnp.float32
BF16 = jnp.bfloat16


def adam_update(current, moment, second, gradient):
    moment_next = BETA_ONE * moment + (1.0 - BETA_ONE) * gradient
    second_next = BETA_TWO * second + (1.0 - BETA_TWO) * gradient * gradient
    corrected = moment_next * (LEARN_RATE / (1.0 - BETA_ONE**STEP))
    spread = jnp.sqrt(second_next * (1.0 / (1.0 - BETA_TWO**STEP)))
    return (current - corrected / (spread + EPSILON), moment_next, second_next)


def contract(left, right, left_dim, right_dim):
    return lax.dot_general(
        left, right, (((left_dim,), (right_dim,)), ((), ())), preferred_element_type=F32
    )


def mid_kernel(group, slots, part_ref, g_ref, f_ref, l_ref, core_ref, moment_ref, second_ref,
               core_out, moment_out, second_out, first_out, last_out,
               grad_wide, first_wide, mix, core_rows, grad_rows, first_wide_terms):
    chunk = pl.program_id(1)
    part = part_ref[0]
    row_id = lax.broadcasted_iota(jnp.int32, (R, LANES), 0)
    lane_id = lax.broadcasted_iota(jnp.int32, (R, LANES), 1)

    @pl.when(chunk == 0)
    def _():
        grads = g_ref[...]
        for a in range(D1):
            for c in range(D3):
                spread = (row_id == a * D2 * D3 + (lane_id % D2) * D3 + c).astype(F32).astype(BF16)
                grad_wide[a * D3 + c] = contract(grads, spread, 1, 0).astype(BF16)
        first_out[...] = jnp.zeros_like(first_out)
        last_out[...] = jnp.zeros_like(last_out)

    for tile in range(LANES):
        core_rows[tile * group:(tile + 1) * group, :] = core_ref[:, tile * R:(tile + 1) * R]
    pick = (row_id == chunk * RCHUNK + lane_id // D2).astype(F32).astype(BF16)
    for a in range(D1):
        first_wide[a] = contract(f_ref[:, a * R:(a + 1) * R], pick, 1, 0)

    for row in range(group):
        own = slice(row * slots, (row + 1) * slots)
        for c in range(D3):
            total = first_wide[0, own] * grad_wide[c, own].astype(F32)
            for a in range(1, D1):
                total += first_wide[a, own] * grad_wide[a * D3 + c, own].astype(F32)
            mix[row, c] = total.astype(BF16)
        first_mix = mix[row].reshape(D3 * slots, LANES)
        last_rows = jnp.concatenate(
            [l_ref[own, c * R:(c + 1) * R] for c in range(D3)], axis=0
        )
        grad_rows[pl.ds(row, LANES, stride=group), :] = contract(first_mix, last_rows, 0, 0)
        core_row = core_rows[pl.ds(row, LANES, stride=group), :].astype(BF16)
        tail = contract(last_rows, core_row, 1, 1)
        terms = grad_wide[part * D3, own].astype(F32) * tail[:slots]
        for c in range(1, D3):
            terms += (
                grad_wide[part * D3 + c, own].astype(F32) * tail[c * slots:(c + 1) * slots]
            )
        first_wide_terms[own, :] = terms.astype(BF16)
        last_out[own, :] += contract(mix[row, part], core_row, 1, 0)
    first_out[...] += contract(first_wide_terms[...], pick, 1, 1)

    for tile in range(LANES):
        cols = slice(tile * R, (tile + 1) * R)
        core_next, moment_next, second_next = adam_update(
            core_ref[:, cols], moment_ref[:, cols], second_ref[:, cols],
            grad_rows[tile * group:(tile + 1) * group, :],
        )
        core_out[:, cols] = core_next
        moment_out[:, cols] = moment_next
        second_out[:, cols] = second_next


def mid_step(part, grads, firsts, lasts, core, moment, second):
    rows, columns = core.shape
    slots = grads.shape[0] // rows
    group = min(GROUP_ROWS, rows)
    held = group * slots
    chunks = R // RCHUNK
    state = pl.BlockSpec((group, RCHUNK * D2 * R), lambda g, j: (g, j))
    terms = pl.BlockSpec((held, R), lambda g, j: (g, 0))
    wide = pl.BlockSpec((held, D1 * R), lambda g, j: (g, 0))
    return pl.pallas_call(
        lambda *refs: mid_kernel(group, slots, *refs),
        grid=(rows // group, chunks),
        in_specs=[
            pl.BlockSpec(memory_space=pltpu.SMEM), terms, wide, wide, state, state, state,
        ],
        out_specs=[state, state, state, terms, terms],
        out_shape=[jax.ShapeDtypeStruct((rows, columns), F32)] * 3
        + [jax.ShapeDtypeStruct((rows * slots, R), F32)] * 2,
        scratch_shapes=[
            pltpu.VMEM((D1 * D3, held, LANES), BF16),
            pltpu.VMEM((D1, held, LANES), F32),
            pltpu.VMEM((group, D3, slots, LANES), BF16),
            pltpu.VMEM((LANES * group, R), F32),
            pltpu.VMEM((LANES * group, R), F32),
            pltpu.VMEM((held, LANES), BF16),
        ],
        compiler_params=pltpu.CompilerParams(vmem_limit_bytes=56 * 1024 * 1024),
    )(part, grads, firsts, lasts, core, moment, second)


def local(
    first_core, first_moment, first_second,
    mid_core, mid_moment, mid_second,
    last_core, last_moment, last_second,
    cotangent, bag_lengths, first_digit, mid_digit, last_digit,
):
    dp_count = lax.axis_size("dp")
    rep_count = lax.axis_size("rep")
    local_rows = mid_core.shape[0]
    block_samples, embed_dim = cotangent.shape
    look_count = first_digit.shape[0]
    outer_rows = first_core.shape[0] * dp_count

    positions = jnp.arange(look_count, dtype=jnp.int32)
    samples = jnp.arange(block_samples, dtype=jnp.int32)
    bag_ends = jnp.sum(
        jnp.where(samples[None, :] <= samples[:, None], bag_lengths[0][None, :], 0), axis=1
    )
    sample_of = jnp.sum((bag_ends[:, None] <= positions[None, :]).astype(jnp.int32), axis=0)
    pieces = jnp.stack(
        [
            mid_digit[:, 0],
            first_digit // 2,
            last_digit // 2,
            sample_of * 4 + (first_digit % 2) * 2 + last_digit % 2,
        ]
    )
    packed = jnp.concatenate([cotangent, pieces.astype(BF16).reshape(-1, embed_dim)], axis=0)

    column = jnp.arange(R * D3, dtype=jnp.int32)
    reorder = ((column[:, None] % D3) * R + column[:, None] // D3 == column[None, :]).astype(F32)
    last_wide = jnp.dot(
        last_core.astype(BF16), reorder.astype(BF16), preferred_element_type=F32
    ).astype(BF16)
    local_cores = jnp.concatenate([first_core.astype(BF16), last_wide], axis=1)
    tiles = (D1 + D3) // rep_count
    share = lax.dynamic_slice_in_dim(local_cores, lax.axis_index("rep") * (tiles * R), tiles * R, 1)
    packed_rows = packed.shape[0]
    message = jnp.concatenate(
        [packed] + [share[:, n * R : (n + 1) * R] for n in range(tiles)], axis=0
    )
    message = jnp.broadcast_to(message[None], (dp_count, *message.shape))
    message = lax.all_to_all(message, "dp", split_axis=0, concat_axis=0, tiled=True)
    message = lax.all_gather(message, "rep", axis=0, tiled=False)
    packed_all = message[:, :, :packed_rows].reshape(-1, packed_rows, embed_dim)
    core_rows = message[:, :, packed_rows:].reshape(rep_count, dp_count, tiles, -1, R)
    cores = jnp.concatenate(
        [
            core_rows[q, :, n].reshape(outer_rows, R)
            for q in range(rep_count)
            for n in range(tiles)
        ],
        axis=1,
    )

    blocks = packed_all.shape[0]
    grads_all = packed_all[:, :block_samples].reshape(blocks * block_samples, embed_dim)
    numbers = packed_all[:, block_samples:].reshape(blocks, 4, look_count).astype(jnp.int32)
    rest = numbers[:, 3]
    keys = (
        (rest // 4) * (outer_rows * outer_rows)
        + (numbers[:, 1] * 2 + (rest // 2) % 2) * outer_rows
        + numbers[:, 2] * 2 + rest % 2
    )
    own_digits = lax.axis_index("dp") * local_rows + jnp.arange(local_rows, dtype=jnp.int32)
    match = numbers[:, 0][None] == own_digits[:, None, None]
    big = jnp.int32(2**30)
    low = jnp.min(jnp.where(match, keys[None], big), axis=2)
    high = jnp.max(jnp.where(match, keys[None], -1), axis=2)
    count = jnp.sum(match.astype(jnp.int32), axis=2)
    slot_keys = jnp.concatenate([jnp.where(count >= 1, low, -1), jnp.where(count >= 2, high, -1)], 1)
    slot_block = jnp.arange(CAP * blocks, dtype=jnp.int32) % blocks
    valid = slot_keys >= 0
    slot_keys = jnp.maximum(slot_keys, 0)
    slot_sample = jnp.where(
        valid, slot_keys // (outer_rows * outer_rows) + slot_block[None, :] * block_samples, -1
    ).reshape(-1)
    slot_first = ((slot_keys // outer_rows) % outer_rows).reshape(-1)
    slot_last = (slot_keys % outer_rows).reshape(-1)

    def one_hot(index, size):
        return (index[:, None] == jnp.arange(size, dtype=jnp.int32)[None, :]).astype(BF16)

    first_hot = one_hot(slot_first, outer_rows)
    last_hot = one_hot(slot_last, outer_rows)
    grads = jnp.dot(
        one_hot(slot_sample, blocks * block_samples), grads_all, preferred_element_type=F32
    ).astype(BF16)
    firsts = jnp.dot(first_hot, cores[:, : D1 * R], preferred_element_type=F32).astype(BF16)
    lasts = jnp.dot(last_hot, cores[:, D1 * R :], preferred_element_type=F32).astype(BF16)

    part = lax.axis_index("rep").astype(jnp.int32).reshape(1)
    core_next, moment_next, second_next, first_terms, last_terms = mid_step(
        part, grads, firsts, lasts, mid_core, mid_moment, mid_second
    )
    partial = jnp.concatenate(
        [
            contract(first_hot, first_terms.astype(BF16), 0, 0),
            contract(last_hot, last_terms.astype(BF16), 0, 0),
        ],
        axis=1,
    ).astype(BF16)
    partial = partial.reshape(dp_count, outer_rows // dp_count, 2 * R)
    arrived = lax.all_to_all(partial, "dp", split_axis=0, concat_axis=0, tiled=True)
    summed = jnp.sum(arrived.astype(F32), axis=0)
    whole = lax.all_gather(summed, "rep", axis=0, tiled=False)
    first_grad = jnp.concatenate([whole[q, :, :R] for q in range(rep_count)], axis=1)
    last_grad = lax.dot_general(
        jnp.concatenate([whole[q, :, R:] for q in range(rep_count)], axis=1),
        reorder,
        (((1,), (1,)), ((), ())),
        precision=lax.Precision.HIGHEST,
        preferred_element_type=F32,
    )
    first_next = adam_update(first_core, first_moment, first_second, first_grad)
    last_next = adam_update(last_core, last_moment, last_second, last_grad)
    return (*first_next, core_next, moment_next, second_next, *last_next)


def solution(mesh):
    core = P("dp", None)
    both = P(("rep", "dp"), None)
    return jax.shard_map(
        local,
        mesh=mesh,
        in_specs=(core,) * 9 + (both, both, P(("rep", "dp")), both, P(("rep", "dp"))),
        out_specs=(core,) * 9,
        check_vma=False,
    )
```
